32 devices in a mesh: groups: 2 (over y), row: 4 (over z), col: 4 (over x, core).
Axes of the slice: x: 2, y: 2, z: 4, core: 2. Of those that a mesh axis runs over, the one named last changes fastest.
Arguments:
- object_slices: bfloat16 [2, 2, 1024, 512], P(None, None, ('groups', 'row'), 'col'), parts along dimension 2, may hold values from -4 to 4
- probe: float32 [2, 384, 384], replicated, may hold values from -5 to 5
- measured: float32 [8, 4, 1, 384, 384], P(('groups', 'row'), 'col'), parts along dimension 0, may hold values from 0 to 2
- offsets: int32 [8, 4, 1, 2], P(('groups', 'row'), 'col'), parts along dimension 0, may hold values from 0 to 127
- owned: int32 [8, 4], P(('groups', 'row'), 'col'), parts along dimension 0, may hold values 0 or 1
Outputs:
- gradient: float32 [2, 2, 1024, 512], P(None, None, ('groups', 'row'), 'col'), parts along dimension 2
The draws below stay inside these ranges and needn't reach their ends.
There are 2 independent parts, one for each index of `groups`. The reference program is written for one: setup_inputs(seed, part) draws one part's arguments, and reference() takes and returns one part's arrays. A program takes and returns all parts, laid end to end along the dimension named above; an argument that names none is the same for every part. Nothing has to cross between parts.
All inputs are finite; a program needn't handle non-finite values. No bound on the sum of `owned` on one device may be relied on, other than what follows from the above.
Results may differ from the reference program's by a relative error of at most 0.0065.
Values may be sent and summed in bfloat16 or wider, within the bound.
A program may use at most 64 MiB of HBM per device.

```python
import math
import jax
import jax.numpy as jnp
from jax import lax

TILE = 128
PROBE = 384
POS_DEV = 1
ROWS = 512
COLS = 512
N_ROW = 4
N_COL = 4


def touch_ends(array, rng, least, largest):
    extent = array.shape
    spot = [jax.random.randint(jax.random.fold_in(rng, axis), (), 0, extent[axis]) for axis in range(len(extent))]
    array = array.at[tuple(spot)].set(least)
    longest = extent.index(max(extent))
    spot[longest] = (spot[longest] + 1) % extent[longest]
    return array.at[tuple(spot)].set(largest)


def steps_of(own_key, dims, cuts, smallest, largest):
    level = 1.0
    for position, blocks in cuts:
        draws = jax.random.uniform(jax.random.fold_in(jax.random.fold_in(own_key, 6), position), (blocks,), jnp.float32, smallest / len(cuts), largest / len(cuts))
        level = level * jnp.repeat(jnp.exp(draws), dims[position] // blocks).reshape((-1,) + (1,) * (len(dims) - 1 - position))
    return level


def noise(stream_key, shape, scale, most, shards=(), kind=jnp.bfloat16):
    drawn = scale * jax.random.normal(stream_key, shape, jnp.float32)
    if shards:
        drawn = drawn * steps_of(stream_key, shape, shards, -0.22, 0.18)
    return jnp.clip(drawn, -most, most).astype(kind)


def setup_inputs(seed: int = 0, part: int = 0) -> dict:
    streams_of = jax.random.split(jax.random.key(seed), 6)
    part_splits = jax.random.split(jax.random.fold_in(streams_of[5], part), 6)
    object_slices = noise(part_splits[0], (2, 2, ROWS, COLS), 1.0, 4.0, ((2, 4), (3, 4)))
    probe = noise(streams_of[1], (2, PROBE, PROBE), 1.0, 5.0, (), jnp.float32)
    measured = jnp.clip(2.0 * jax.random.uniform(part_splits[2], (N_ROW, N_COL, POS_DEV, PROBE, PROBE), jnp.float32) ** steps_of(part_splits[2], (N_ROW, N_COL, POS_DEV, PROBE, PROBE), ((0, 4), (1, 4)), -0.2, 0.2), 0.0, 2.0)
    offsets = touch_ends(jax.random.randint(part_splits[3], (N_ROW, N_COL, POS_DEV, 2), 0, TILE), jax.random.fold_in(part_splits[3], 1), 0, TILE - 1).astype(jnp.int32)
    owned = touch_ends((jax.random.randint(part_splits[4], (N_ROW, N_COL), 0, 4) < 3).astype(jnp.int32), jax.random.fold_in(part_splits[4], 1), 0, 1)
    return {"object_slices": object_slices, "probe": probe, "measured": measured, "offsets": offsets, "owned": owned}


def make_tables(length):
    counter = jnp.arange(length, dtype=jnp.int32)
    differ = (counter[:, None] - counter[None, :]) % length
    chirp = (differ * differ % (2 * length)).astype(jnp.float32) * (math.pi / length)
    product = counter[:, None] * counter[None, :] % length
    fourier = product.astype(jnp.float32) * (-2.0 * math.pi / length)
    scaling = 1.0 / math.sqrt(length)
    return ((jnp.cos(chirp) * scaling).astype(jnp.bfloat16), (jnp.sin(chirp) * scaling).astype(jnp.bfloat16), (jnp.cos(fourier) * scaling).astype(jnp.bfloat16), (jnp.sin(fourier) * scaling).astype(jnp.bfloat16))

def matmul_wide(left, right):
    return jnp.dot(left.astype(jnp.float32), right.astype(jnp.float32), precision=lax.Precision.HIGHEST)

def transform(wave_re, wave_im, table_re, table_im, parity):
    wave_re, wave_im = lax.optimization_barrier((wave_re, wave_im))
    half_re = (matmul_wide(table_re, wave_re) - parity * matmul_wide(table_im, wave_im)).astype(jnp.bfloat16)
    half_im = (matmul_wide(table_re, wave_im) + parity * matmul_wide(table_im, wave_re)).astype(jnp.bfloat16)
    half_re, half_im = lax.optimization_barrier((half_re, half_im))
    out_re = matmul_wide(half_re, table_re) - parity * matmul_wide(half_im, table_im)
    out_im = matmul_wide(half_im, table_re) + parity * matmul_wide(half_re, table_im)
    return (out_re, out_im)

def position_grad(patch, probe_re, probe_im, measure, tables):
    chirp_re, chirp_im, four_re, four_im = tables
    first_re, first_im, second_re, second_im = (patch[0, 0], patch[0, 1], patch[1, 0], patch[1, 1])
    psi_re = (probe_re * first_re - probe_im * first_im).astype(jnp.bfloat16)
    psi_im = (probe_re * first_im + probe_im * first_re).astype(jnp.bfloat16)
    phi_re, phi_im = transform(psi_re, psi_im, chirp_re, chirp_im, 1.0)
    exit_re = (phi_re * second_re - phi_im * second_im).astype(jnp.bfloat16)
    exit_im = (phi_re * second_im + phi_im * second_re).astype(jnp.bfloat16)
    wave_re, wave_im = transform(exit_re, exit_im, four_re, four_im, 1.0)
    magnitude = jnp.maximum(jnp.sqrt(wave_re * wave_re + wave_im * wave_im), 0.5)
    ratio = measure / magnitude
    resid_re = (wave_re - ratio * wave_re).astype(jnp.bfloat16)
    resid_im = (wave_im - ratio * wave_im).astype(jnp.bfloat16)
    back_re, back_im = transform(resid_re, resid_im, four_re, four_im, -1.0)
    grad_two_re = phi_re * back_re + phi_im * back_im
    grad_two_im = phi_re * back_im - phi_im * back_re
    gphi_re = (second_re * back_re + second_im * back_im).astype(jnp.bfloat16)
    gphi_im = (second_re * back_im - second_im * back_re).astype(jnp.bfloat16)
    front_re, front_im = transform(gphi_re, gphi_im, chirp_re, chirp_im, -1.0)
    grad_one_re = probe_re * front_re + probe_im * front_im
    grad_one_im = probe_re * front_im - probe_im * front_re
    return jnp.stack([jnp.stack([grad_one_re, grad_one_im]), jnp.stack([grad_two_re, grad_two_im])])

def reference(object_slices, probe, measured, offsets, owned):
    tables = make_tables(PROBE)
    padded = jnp.pad(object_slices.astype(jnp.float32), ((0, 0), (0, 0), (2 * TILE, 2 * TILE), (2 * TILE, 2 * TILE)))
    tile_rows = jnp.broadcast_to(jnp.arange(N_ROW, dtype=jnp.int32)[:, None, None], (N_ROW, N_COL, POS_DEV)).reshape(-1)
    tile_cols = jnp.broadcast_to(jnp.arange(N_COL, dtype=jnp.int32)[None, :, None], (N_ROW, N_COL, POS_DEV)).reshape(-1)
    flat_offsets = offsets.reshape(-1, 2).astype(jnp.int32)
    flat_measured = measured.reshape(-1, PROBE, PROBE)

    def one_step(carried, inputs):
        tile_row, tile_col, offset_pair, measure = inputs
        row_start = (tile_row * TILE + 2 * TILE - PROBE // 2 + offset_pair[0]).astype(jnp.int32)
        col_start = (tile_col * TILE + 2 * TILE - PROBE // 2 + offset_pair[1]).astype(jnp.int32)
        zero_index = jnp.zeros((), jnp.int32)
        starts = (zero_index, zero_index, row_start, col_start)
        patch = lax.dynamic_slice(padded, starts, (2, 2, PROBE, PROBE))
        grads = position_grad(patch, probe[0], probe[1], measure, tables)
        current = lax.dynamic_slice(carried, starts, (2, 2, PROBE, PROBE))
        return (lax.dynamic_update_slice(carried, current + grads, starts), None)
    total, _ = lax.scan(one_step, jnp.zeros(padded.shape, jnp.float32), (tile_rows, tile_cols, flat_offsets, flat_measured))
    cropped = total[:, :, 2 * TILE:2 * TILE + ROWS, 2 * TILE:2 * TILE + COLS]
    tile_mask = jnp.repeat(jnp.repeat(owned, TILE, axis=0), TILE, axis=1).astype(jnp.float32)
    return cropped * tile_mask[None, None]
```

```python
import functools
import math

import jax
import jax.numpy as jnp
import numpy as np
from jax import lax
from jax.experimental import pallas as pl
from jax.experimental.pallas import tpu as pltpu
from jax.sharding import PartitionSpec as P

MESH = pl.DeviceIdType.MESH
F32 = jnp.float32
BF16 = jnp.bfloat16
STEPS = (-2, -1, 1, 2)


def make_tables(length):
    counter = np.arange(length, dtype=np.int32)
    differ = (counter[:, None] - counter[None, :]) % length
    chirp = (differ * differ % (2 * length)).astype(np.float32) * np.float32(math.pi / length)
    product = counter[:, None] * counter[None, :] % length
    fourier = product.astype(np.float32) * np.float32(-2.0 * math.pi / length)
    scaling = np.float32(1.0 / math.sqrt(length))
    parts = (np.cos(chirp), np.sin(chirp), np.cos(fourier), np.sin(fourier))
    return [jnp.asarray(part * scaling, BF16) for part in parts]


def kernel(
    n_row, n_col, tile, length,
    offs_ref, owned_ref, obj_ref, probe_ref, meas_ref, hre_ref, him_ref, fre_ref, fim_ref,
    out_ref,
    region, recv_pack, send_pack, chirp_w, chirp_c, left_f, left_b, right_f, right_b,
    prolled, stacked, halves, phi, second, gsend, gown, gpack, crecv, cpack, dsend, down, drecv,
    dhalf, send_sem, recv_sem,
):
    row = lax.axis_index("row")
    col = lax.axis_index("col")
    half = tile // 2
    n = length
    rows_all = 4 * tile
    spot = {"row": (row, n_row), "col": (col, n_col)}

    def has(axis, step):
        at, count = spot[axis]
        return jnp.logical_and(at + step >= 0, at + step < count)

    barrier = pltpu.get_barrier_semaphore()
    peers = jnp.int32(0)
    for axis in ("row", "col"):
        for step in STEPS:
            there = has(axis, step)
            peers = peers + there.astype(jnp.int32)

            @pl.when(there)
            def _(axis=axis, step=step):
                pl.semaphore_signal(
                    barrier, inc=1, device_id={axis: spot[axis][0] + step}, device_id_type=MESH
                )

    pl.semaphore_wait(barrier, peers)

    def endpoints(phase, s):
        if phase == 0:
            ends = (
                (obj_ref.at[s, :, 0:half], region.at[s, 1, :, 3 * tile:3 * tile + half]),
                (obj_ref.at[s], region.at[s, 1, :, 2 * tile:3 * tile]),
                (obj_ref.at[s], region.at[s, 1, :, 0:tile]),
                (obj_ref.at[s, :, half:tile], region.at[s, 1, :, 3 * tile + half:4 * tile]),
            )
        elif phase == 1:
            ends = (
                (send_pack.at[s, 1], recv_pack.at[s, 0]),
                (region.at[s, 1], region.at[s, 2]),
                (region.at[s, 1], region.at[s, 0]),
                (send_pack.at[s, 0], recv_pack.at[s, 1]),
            )
        elif phase == 2:
            ends = (
                (gpack.at[s, 1], cpack.at[s, 1]),
                (gsend.at[s, 0], crecv.at[s, 0]),
                (gsend.at[s, 1], crecv.at[s, 1]),
                (gpack.at[s, 0], cpack.at[s, 0]),
            )
        else:
            ends = (
                (dsend.at[s, :, 3 * tile + half:4 * tile], dhalf.at[s, 1]),
                (dsend.at[s, :, 0:tile], drecv.at[s, 0]),
                (dsend.at[s, :, 2 * tile:3 * tile], drecv.at[s, 1]),
                (dsend.at[s, :, 3 * tile:3 * tile + half], dhalf.at[s, 0]),
            )
        return "col" if phase in (1, 2) else "row", ends

    def descriptors(phase, s):
        axis, ends = endpoints(phase, s)
        made = []
        for k, step in enumerate(STEPS):
            made.append(
                pltpu.make_async_remote_copy(
                    src_ref=ends[k][0],
                    dst_ref=ends[k][1],
                    send_sem=send_sem.at[phase, s, k],
                    recv_sem=recv_sem.at[phase, s, k],
                    device_id={axis: spot[axis][0] + step},
                    device_id_type=MESH,
                )
            )
        return axis, made

    def start(phase, s):
        axis, made = descriptors(phase, s)
        for step, copy in sorted(zip(STEPS, made), key=lambda pair: -abs(pair[0])):
            @pl.when(has(axis, step))
            def _(copy=copy):
                copy.start()

    def wait_recv(phase, s):
        axis, made = descriptors(phase, s)
        for k, step in enumerate(STEPS):
            @pl.when(has(axis, -step))
            def _(copy=made[k]):
                copy.wait_recv()

    def wait_send(phase, s):
        axis, made = descriptors(phase, s)
        for step, copy in zip(STEPS, made):
            @pl.when(has(axis, step))
            def _(copy=copy):
                copy.wait_send()

    def clear(phase, s):
        axis, ends = endpoints(phase, s)
        for k, step in enumerate(STEPS):
            @pl.when(jnp.logical_not(has(axis, -step)))
            def _(target=ends[k][1]):
                target[...] = jnp.zeros(target.shape, target.dtype)

    start(0, 0)
    start(0, 1)
    for phase in range(4):
        for s in range(2):
            clear(phase, s)

    u = offs_ref[0]
    v = offs_ref[1]
    shift_u = lax.rem(u + n - half, n)
    shift_v = lax.rem(v + n - half, n)

    def pack(re, im, left):
        lane = lax.broadcasted_iota(jnp.int32, re.shape, 1)
        moved = pltpu.roll(im, half, 1)
        return jnp.where(lane < half, re, moved) if left else jnp.where(lane < half, moved, re)

    def unpack(packed):
        return packed, pltpu.roll(packed, half, 1)

    region[0, 1, :, tile:2 * tile] = obj_ref[0]
    region[1, 1, :, tile:2 * tile] = obj_ref[1]

    def second_phase(s):
        wait_recv(0, s)
        re = region[s, 1, 0].astype(F32)
        im = region[s, 1, 1].astype(F32)
        send_pack[s, 0] = pack(re, im, False).astype(BF16)
        send_pack[s, 1] = pack(re, im, True).astype(BF16)
        start(1, s)

    def fill(target, a, b, c, d):
        target[0:n, 0:n] = a
        target[0:n, n:2 * n] = b
        target[n:2 * n, 0:n] = c
        target[n:2 * n, n:2 * n] = d

    for k in range(2):
        prolled[k] = pltpu.roll(pltpu.roll(probe_ref[k], shift_u, 0), shift_v, 1)
    second_phase(0)
    hre, him = hre_ref[...], him_ref[...]
    fill(chirp_w, hre, him, -him, hre)
    fill(chirp_c, hre, -him, him, hre)
    second_phase(1)
    fre, fim = fre_ref[...].astype(F32), fim_ref[...].astype(F32)

    def rolled(shift, axis):
        return pltpu.roll(fre, shift, axis).astype(BF16), pltpu.roll(fim, shift, axis).astype(BF16)

    re, im = rolled(shift_u, 1)
    fill(left_f, re, -im, im, re)
    re, im = rolled(shift_u, 0)
    fill(left_b, re, im, -im, re)
    re, im = rolled(shift_v, 0)
    fill(right_f, re, im, -im, re)
    re, im = rolled(shift_v, 1)
    fill(right_b, re, -im, im, re)

    row_half = lax.broadcasted_iota(jnp.int32, (half, tile), 0)
    lane_full = lax.broadcasted_iota(jnp.int32, (n, tile), 1)
    near_top = row_half >= u - half
    near_bottom = row_half + (n - half) < u + n - half
    near_left = lane_full >= v - half
    near_right = lane_full + 2 * tile < v + n - half

    def pick_rows(x):
        x = x.astype(F32)
        top = jnp.where(near_top, x[0:half], x[n:n + half])
        bottom = jnp.where(near_bottom, x[n - half:n], x[n + half:n + tile])
        return jnp.concatenate([top, x[half:n - half], bottom], axis=0)

    def spread_rows(x):
        top, bottom = x[0:half], x[n - half:n]
        zero = jnp.zeros_like(top)
        return jnp.concatenate(
            [
                jnp.where(near_top, top, zero), x[half:n - half], jnp.where(near_bottom, bottom, zero),
                jnp.where(near_top, zero, top), jnp.where(near_bottom, zero, bottom),
            ],
            axis=0,
        )

    def window(s):
        left_alt = unpack(pick_rows(recv_pack[s, 0]))
        right_alt = unpack(pick_rows(recv_pack[s, 1]))
        made = []
        for k in range(2):
            made.append((
                jnp.where(near_left, pick_rows(region[s, 0, k]), left_alt[k]),
                pick_rows(region[s, 1, k]),
                jnp.where(near_right, pick_rows(region[s, 2, k]), right_alt[k]),
            ))
        return made

    def left_mul(table):
        product = jnp.dot(table[...], stacked[...], preferred_element_type=F32)
        halves[:, 0:n] = product[0:n].astype(BF16)
        halves[:, n:2 * n] = product[n:2 * n].astype(BF16)

    def right_mul(table):
        product = jnp.dot(halves[...], table[...], preferred_element_type=F32)
        return product[:, 0:n], product[:, n:2 * n]

    def scatter_start(s, grad_re, grad_im):
        lefts, rights = [], []
        for k, grad in enumerate((grad_re, grad_im)):
            first, mid, last = grad[:, 0:tile], grad[:, tile:2 * tile], grad[:, 2 * tile:n]
            zero = jnp.zeros_like(first)
            gsend[s, 0, k] = spread_rows(jnp.where(near_left, first, zero)).astype(BF16)
            gsend[s, 1, k] = spread_rows(jnp.where(near_right, last, zero)).astype(BF16)
            gown[s, k] = spread_rows(mid)
            lefts.append(jnp.where(near_left, zero, first))
            rights.append(jnp.where(near_right, zero, last))
        gpack[s, 0] = spread_rows(pack(lefts[0], lefts[1], True)).astype(BF16)
        gpack[s, 1] = spread_rows(pack(rights[0], rights[1], False)).astype(BF16)
        start(2, s)

    def scatter_rows(s):
        wait_recv(2, s)
        lane = lax.broadcasted_iota(jnp.int32, (rows_all, tile), 1)
        lefts = unpack(cpack[s, 0].astype(F32))
        rights = unpack(cpack[s, 1].astype(F32))
        for k in range(2):
            total = gown[s, k] + crecv[s, 0, k].astype(F32) + crecv[s, 1, k].astype(F32)
            total = total + jnp.where(lane < half, lefts[k], rights[k])
            dsend[s, k] = total.astype(BF16)
            down[s, k] = total[tile:2 * tile]
        start(3, s)

    def finish(s):
        wait_recv(3, s)
        keep = owned_ref[0].astype(F32)
        for k in range(2):
            total = down[s, k] + drecv[s, 0, k].astype(F32) + drecv[s, 1, k].astype(F32)
            ends = jnp.concatenate([dhalf[s, 0, k], dhalf[s, 1, k]], axis=0).astype(F32)
            out_ref[s, k] = (total + ends) * keep

    wait_recv(1, 0)
    first_re, first_im = window(0)
    for k in range(3):
        lanes = slice(k * tile, (k + 1) * tile)
        probe_re, probe_im = prolled[0, :, lanes], prolled[1, :, lanes]
        a, b = first_re[k], first_im[k]
        stacked[0:n, lanes] = (probe_re * a - probe_im * b).astype(BF16)
        stacked[n:2 * n, lanes] = (probe_re * b + probe_im * a).astype(BF16)
    left_mul(chirp_c)
    phi_re, phi_im = right_mul(chirp_w)
    phi[0], phi[1] = phi_re, phi_im
    wait_recv(1, 1)
    second_re, second_im = window(1)
    for k in range(3):
        lanes = slice(k * tile, (k + 1) * tile)
        second[0, :, lanes], second[1, :, lanes] = second_re[k], second_im[k]
        a, b = second_re[k], second_im[k]
        p, q = phi[0, :, lanes], phi[1, :, lanes]
        stacked[0:n, lanes] = (p * a - q * b).astype(BF16)
        stacked[n:2 * n, lanes] = (p * b + q * a).astype(BF16)
    left_mul(left_f)
    wave_re, wave_im = right_mul(right_f)
    power = wave_re * wave_re + wave_im * wave_im
    ratio = meas_ref[...] * lax.rsqrt(jnp.maximum(power, 0.25))
    stacked[0:n] = (wave_re - ratio * wave_re).astype(BF16)
    stacked[n:2 * n] = (wave_im - ratio * wave_im).astype(BF16)
    left_mul(left_b)
    back_re, back_im = right_mul(right_b)
    p, q = phi[0], phi[1]
    scatter_start(1, p * back_re + q * back_im, p * back_im - q * back_re)
    a, b = second[0], second[1]
    stacked[0:n] = (a * back_re + b * back_im).astype(BF16)
    stacked[n:2 * n] = (a * back_im - b * back_re).astype(BF16)
    left_mul(chirp_w)
    front_re, front_im = right_mul(chirp_c)
    p, q = prolled[0], prolled[1]
    scatter_start(0, p * front_re + q * front_im, p * front_im - q * front_re)
    scatter_rows(1)
    scatter_rows(0)
    finish(1)
    finish(0)
    for phase in range(4):
        for s in range(2):
            wait_send(phase, s)


def shards(n_row, n_col, object_slices, probe, measured, offsets, owned):
    tile = object_slices.shape[2]
    length = probe.shape[1]
    tables = make_tables(length)
    rows_all = 4 * tile
    vmem = pl.BlockSpec(memory_space=pltpu.VMEM)
    smem = pl.BlockSpec(memory_space=pltpu.SMEM)
    wide = pltpu.VMEM((2 * length, 2 * length), BF16)
    packs = pltpu.VMEM((2, 2, rows_all, tile), BF16)
    return pl.pallas_call(
        functools.partial(kernel, n_row, n_col, tile, length),
        out_shape=jax.ShapeDtypeStruct(object_slices.shape, F32),
        in_specs=[smem, smem] + [vmem] * 7,
        out_specs=vmem,
        scratch_shapes=[
            pltpu.VMEM((2, 3, 2, rows_all, tile), BF16),
            packs, packs,
            wide, wide, wide, wide, wide, wide,
            pltpu.VMEM((2, length, length), F32),
            pltpu.VMEM((2 * length, length), BF16),
            pltpu.VMEM((length, 2 * length), BF16),
            pltpu.VMEM((2, length, length), F32),
            pltpu.VMEM((2, length, length), F32),
            pltpu.VMEM((2, 2, 2, rows_all, tile), BF16),
            pltpu.VMEM((2, 2, rows_all, tile), F32),
            packs,
            pltpu.VMEM((2, 2, 2, rows_all, tile), BF16),
            packs, packs,
            pltpu.VMEM((2, 2, tile, tile), F32),
            pltpu.VMEM((2, 2, 2, tile, tile), BF16),
            pltpu.VMEM((2, 2, 2, tile // 2, tile), BF16),
            pltpu.SemaphoreType.DMA((4, 2, 4)),
            pltpu.SemaphoreType.DMA((4, 2, 4)),
        ],
        compiler_params=pltpu.CompilerParams(
            collective_id=0, has_side_effects=True, vmem_limit_bytes=50 * 1024 * 1024
        ),
    )(
        offsets.reshape(2), owned.reshape(1), object_slices, probe,
        measured.reshape(length, length), *tables,
    )


def solution(mesh):
    in_specs = (
        P(None, None, ("groups", "row"), "col"),
        P(),
        P(("groups", "row"), "col", None, None, None),
        P(("groups", "row"), "col", None, None),
        P(("groups", "row"), "col"),
    )
    out_specs = P(None, None, ("groups", "row"), "col")
    body = functools.partial(shards, mesh.shape["row"], mesh.shape["col"])
    return jax.shard_map(body, mesh=mesh, in_specs=in_specs, out_specs=out_specs, check_vma=False)
```

```python
import functools
import math

import jax
import jax.numpy as jnp
import numpy as np
from jax import lax
from jax.experimental import pallas as pl
from jax.experimental.pallas import tpu as pltpu
from jax.sharding import PartitionSpec as P

MESH = pl.DeviceIdType.MESH
F32 = jnp.float32
BF16 = jnp.bfloat16
STEPS = (-2, -1, 1, 2)


def make_tables(length):
    counter = np.arange(length, dtype=np.int32)
    differ = (counter[:, None] - counter[None, :]) % length
    chirp = (differ * differ % (2 * length)).astype(np.float32) * np.float32(math.pi / length)
    product = counter[:, None] * counter[None, :] % length
    fourier = product.astype(np.float32) * np.float32(-2.0 * math.pi / length)
    scaling = np.float32(1.0 / math.sqrt(length))
    parts = (np.cos(chirp), np.sin(chirp), np.cos(fourier), np.sin(fourier))
    return jnp.asarray(np.stack(parts) * scaling, BF16)


def kernel(
    n_row, n_col, tile, length,
    offs_ref, owned_ref, obj_ref, probe_hbm, meas_hbm, tables_hbm,
    out_ref,
    probe_ref, meas_ref, tables_ref, region, recv_pack, send_pack, chirp_w, chirp_c, left_f, left_b, right_f, right_b,
    prolled, stacked, halves, phi, second, gsend, gown, gpack, crecv, cpack, dsend, down, drecv,
    dhalf, send_sem, recv_sem, load_sem,
):
    row = lax.axis_index("row")
    col = lax.axis_index("col")
    half = tile // 2
    n = length
    rows_all = 4 * tile
    spot = {"row": (row, n_row), "col": (col, n_col)}

    def has(axis, step):
        at, count = spot[axis]
        return jnp.logical_and(at + step >= 0, at + step < count)

    loads = [
        pltpu.make_async_copy(src, dst, load_sem.at[k])
        for k, (src, dst) in enumerate((
            (obj_ref.at[0], region.at[0, 1, :, tile:2 * tile]),
            (obj_ref.at[1], region.at[1, 1, :, tile:2 * tile]),
            (probe_hbm, probe_ref),
            (tables_hbm, tables_ref),
            (meas_hbm.at[0, 0, 0], meas_ref),
        ))
    ]
    for load in loads:
        load.start()

    barrier = pltpu.get_barrier_semaphore()
    peers = jnp.int32(0)
    for axis in ("row", "col"):
        for step in STEPS:
            there = has(axis, step)
            peers = peers + there.astype(jnp.int32)

            @pl.when(there)
            def _(axis=axis, step=step):
                pl.semaphore_signal(
                    barrier, inc=1, device_id={axis: spot[axis][0] + step}, device_id_type=MESH
                )

    pl.semaphore_wait(barrier, peers)

    def endpoints(phase, s):
        if phase == 0:
            ends = (
                (obj_ref.at[s, :, 0:half], region.at[s, 1, :, 3 * tile:3 * tile + half]),
                (obj_ref.at[s], region.at[s, 1, :, 2 * tile:3 * tile]),
                (obj_ref.at[s], region.at[s, 1, :, 0:tile]),
                (obj_ref.at[s, :, half:tile], region.at[s, 1, :, 3 * tile + half:4 * tile]),
            )
        elif phase == 1:
            ends = (
                (send_pack.at[s, 1], recv_pack.at[s, 0]),
                (region.at[s, 1], region.at[s, 2]),
                (region.at[s, 1], region.at[s, 0]),
                (send_pack.at[s, 0], recv_pack.at[s, 1]),
            )
        elif phase == 2:
            ends = (
                (gpack.at[s, 1], cpack.at[s, 1]),
                (gsend.at[s, 0], crecv.at[s, 0]),
                (gsend.at[s, 1], crecv.at[s, 1]),
                (gpack.at[s, 0], cpack.at[s, 0]),
            )
        else:
            ends = (
                (dsend.at[s, :, 3 * tile + half:4 * tile], dhalf.at[s, 1]),
                (dsend.at[s, :, 0:tile], drecv.at[s, 0]),
                (dsend.at[s, :, 2 * tile:3 * tile], drecv.at[s, 1]),
                (dsend.at[s, :, 3 * tile:3 * tile + half], dhalf.at[s, 0]),
            )
        return "col" if phase in (1, 2) else "row", ends

    def descriptors(phase, s, steps=STEPS):
        axis, ends = endpoints(phase, s)
        made = {}
        for step in steps:
            k = STEPS.index(step)
            made[step] = (
                pltpu.make_async_remote_copy(
                    src_ref=ends[k][0],
                    dst_ref=ends[k][1],
                    send_sem=send_sem.at[phase, s, k],
                    recv_sem=recv_sem.at[phase, s, k],
                    device_id={axis: spot[axis][0] + step},
                    device_id_type=MESH,
                )
            )
        return axis, made

    def start(phase, s, steps=(-2, 2, -1, 1)):
        axis, made = descriptors(phase, s, steps)
        for step in steps:
            copy = made[step]

            @pl.when(has(axis, step))
            def _(copy=copy):
                copy.start()

    def wait_recv(phase, s):
        axis, made = descriptors(phase, s)
        for k, step in enumerate(STEPS):
            @pl.when(has(axis, -step))
            def _(copy=made[step]):
                copy.wait_recv()

    def wait_send(phase, s):
        axis, made = descriptors(phase, s)
        for step, copy in made.items():
            @pl.when(has(axis, step))
            def _(copy=copy):
                copy.wait_send()

    def clear(phase, s):
        axis, ends = endpoints(phase, s)
        for k, step in enumerate(STEPS):
            @pl.when(jnp.logical_not(has(axis, -step)))
            def _(target=ends[k][1]):
                target[...] = jnp.zeros(target.shape, target.dtype)

    start(0, 0)
    for phase in range(2):
        for s in range(2):
            clear(phase, s)

    u = offs_ref[0, 0, 0, 0]
    v = offs_ref[0, 0, 0, 1]
    shift_u = lax.rem(u + n - half, n)
    shift_v = lax.rem(v + n - half, n)

    def pack(re, im, left):
        lane = lax.broadcasted_iota(jnp.int32, re.shape, 1)
        moved = pltpu.roll(im, half, 1)
        return jnp.where(lane < half, re, moved) if left else jnp.where(lane < half, moved, re)

    def unpack(packed):
        return packed, pltpu.roll(packed, half, 1)

    def second_phase(s):
        loads[s].wait()
        wait_recv(0, s)
        re = region[s, 1, 0].astype(F32)
        im = region[s, 1, 1].astype(F32)
        send_pack[s, 0] = pack(re, im, False).astype(BF16)
        send_pack[s, 1] = pack(re, im, True).astype(BF16)
        start(1, s)

    def fill(target, a, b, c, d):
        target[0:n, 0:n] = a
        target[0:n, n:2 * n] = b
        target[n:2 * n, 0:n] = c
        target[n:2 * n, n:2 * n] = d

    loads[2].wait()
    for k in range(2):
        prolled[k] = pltpu.roll(pltpu.roll(probe_ref[k], shift_u, 0), shift_v, 1)
    second_phase(0)
    start(0, 1)
    loads[3].wait()
    hre, him = tables_ref[0], tables_ref[1]
    fill(chirp_w, hre, him, -him, hre)
    fill(chirp_c, hre, -him, him, hre)
    for phase in range(2, 4):
        for s in range(2):
            clear(phase, s)
    fre, fim = tables_ref[2].astype(F32), tables_ref[3].astype(F32)

    def rolled(shift, axis):
        return pltpu.roll(fre, shift, axis).astype(BF16), pltpu.roll(fim, shift, axis).astype(BF16)

    re, im = rolled(shift_u, 1)
    fill(left_f, re, -im, im, re)
    re, im = rolled(shift_u, 0)
    fill(left_b, re, im, -im, re)
    re, im = rolled(shift_v, 0)
    fill(right_f, re, im, -im, re)
    re, im = rolled(shift_v, 1)
    fill(right_b, re, -im, im, re)

    row_half = lax.broadcasted_iota(jnp.int32, (half, tile), 0)
    lane_full = lax.broadcasted_iota(jnp.int32, (n, tile), 1)
    near_top = row_half >= u - half
    near_bottom = row_half + (n - half) < u + n - half
    near_left = lane_full >= v - half
    near_right = lane_full + 2 * tile < v + n - half

    def pick_rows(x):
        x = x.astype(F32)
        top = jnp.where(near_top, x[0:half], x[n:n + half])
        bottom = jnp.where(near_bottom, x[n - half:n], x[n + half:n + tile])
        return jnp.concatenate([top, x[half:n - half], bottom], axis=0)

    def spread_rows(x):
        top, bottom = x[0:half], x[n - half:n]
        zero = jnp.zeros_like(top)
        return jnp.concatenate(
            [
                jnp.where(near_top, top, zero), x[half:n - half], jnp.where(near_bottom, bottom, zero),
                jnp.where(near_top, zero, top), jnp.where(near_bottom, zero, bottom),
            ],
            axis=0,
        )

    def window(s):
        left_alt = unpack(pick_rows(recv_pack[s, 0]))
        right_alt = unpack(pick_rows(recv_pack[s, 1]))
        made = []
        for k in range(2):
            made.append((
                jnp.where(near_left, pick_rows(region[s, 0, k]), left_alt[k]),
                pick_rows(region[s, 1, k]),
                jnp.where(near_right, pick_rows(region[s, 2, k]), right_alt[k]),
            ))
        return made

    def left_mul(table):
        product = jnp.dot(table[...], stacked[...], preferred_element_type=F32)
        halves[:, 0:n] = product[0:n].astype(BF16)
        halves[:, n:2 * n] = product[n:2 * n].astype(BF16)

    def right_mul(table, k):
        columns = [table[:, at:at + tile] for at in (k * tile, n + k * tile)]
        product = jnp.dot(
            halves[...], jnp.concatenate(columns, axis=1), preferred_element_type=F32
        )
        return product[:, 0:tile], product[:, tile:2 * tile]

    def scatter_slot(s, k, grad_re, grad_im):
        if k == 1:
            gown[s, 0], gown[s, 1] = spread_rows(grad_re), spread_rows(grad_im)
            return
        near = near_left if k == 0 else near_right
        zero = jnp.zeros_like(grad_re)
        far = [jnp.where(near, zero, grad) for grad in (grad_re, grad_im)]
        gpack[s, k // 2] = spread_rows(pack(far[0], far[1], k == 0)).astype(BF16)
        for part, grad in enumerate((grad_re, grad_im)):
            gsend[s, k // 2, part] = spread_rows(jnp.where(near, grad, zero)).astype(BF16)
        start(2, s, (2, -1) if k == 0 else (-2, 1))

    def scatter_rows(s):
        wait_recv(2, s)
        lane = lax.broadcasted_iota(jnp.int32, (rows_all, tile), 1)
        lefts = unpack(cpack[s, 0].astype(F32))
        rights = unpack(cpack[s, 1].astype(F32))
        for k in range(2):
            total = gown[s, k] + crecv[s, 0, k].astype(F32) + crecv[s, 1, k].astype(F32)
            total = total + jnp.where(lane < half, lefts[k], rights[k])
            dsend[s, k] = total.astype(BF16)
            down[s, k] = total[tile:2 * tile]
        start(3, s)

    def finish(s):
        wait_recv(3, s)
        keep = owned_ref[0, 0].astype(F32)
        for k in range(2):
            total = down[s, k] + drecv[s, 0, k].astype(F32) + drecv[s, 1, k].astype(F32)
            ends = jnp.concatenate([dhalf[s, 0, k], dhalf[s, 1, k]], axis=0).astype(F32)
            out_ref[s, k] = (total + ends) * keep

    def lanes_of(k):
        return slice(k * tile, (k + 1) * tile)

    def stack(k, re, im):
        stacked[0:n, lanes_of(k)] = re.astype(BF16)
        stacked[n:2 * n, lanes_of(k)] = im.astype(BF16)

    wait_recv(1, 0)
    second_phase(1)
    first_re, first_im = window(0)
    for k in range(3):
        p, q = prolled[0, :, lanes_of(k)], prolled[1, :, lanes_of(k)]
        a, b = first_re[k], first_im[k]
        stack(k, p * a - q * b, p * b + q * a)
    left_mul(chirp_c)
    for k in range(3):
        phi[0, :, lanes_of(k)], phi[1, :, lanes_of(k)] = right_mul(chirp_w, k)
    wait_recv(1, 1)
    second_re, second_im = window(1)
    for k in range(3):
        a, b = second_re[k], second_im[k]
        second[0, :, lanes_of(k)], second[1, :, lanes_of(k)] = a, b
        p, q = phi[0, :, lanes_of(k)], phi[1, :, lanes_of(k)]
        stack(k, p * a - q * b, p * b + q * a)
    left_mul(left_f)
    loads[4].wait()
    for k in range(3):
        wave_re, wave_im = right_mul(right_f, k)
        power = wave_re * wave_re + wave_im * wave_im
        ratio = meas_ref[:, lanes_of(k)] * lax.rsqrt(jnp.maximum(power, 0.25))
        stack(k, wave_re - ratio * wave_re, wave_im - ratio * wave_im)
    left_mul(left_b)
    for k in (0, 2, 1):
        back_re, back_im = right_mul(right_b, k)
        p, q = phi[0, :, lanes_of(k)], phi[1, :, lanes_of(k)]
        scatter_slot(1, k, p * back_re + q * back_im, p * back_im - q * back_re)
        a, b = second[0, :, lanes_of(k)], second[1, :, lanes_of(k)]
        stack(k, a * back_re + b * back_im, a * back_im - b * back_re)
    left_mul(chirp_w)
    for k in (0, 2, 1):
        front_re, front_im = right_mul(chirp_c, k)
        p, q = prolled[0, :, lanes_of(k)], prolled[1, :, lanes_of(k)]
        scatter_slot(0, k, p * front_re + q * front_im, p * front_im - q * front_re)
    scatter_rows(1)
    scatter_rows(0)
    finish(1)
    finish(0)
    for phase in range(4):
        for s in range(2):
            wait_send(phase, s)


def shards(n_row, n_col, object_slices, probe, measured, offsets, owned):
    tile = object_slices.shape[2]
    length = probe.shape[1]
    tables = make_tables(length)
    rows_all = 4 * tile
    vmem = pl.BlockSpec(memory_space=pltpu.VMEM)
    hbm = pl.BlockSpec(memory_space=pltpu.HBM)
    smem = pl.BlockSpec(memory_space=pltpu.SMEM)
    wide = pltpu.VMEM((2 * length, 2 * length), BF16)
    packs = pltpu.VMEM((2, 2, rows_all, tile), BF16)
    return pl.pallas_call(
        functools.partial(kernel, n_row, n_col, tile, length),
        out_shape=jax.ShapeDtypeStruct(object_slices.shape, F32),
        in_specs=[smem, smem] + [hbm] * 4,
        out_specs=vmem,
        scratch_shapes=[
            pltpu.VMEM((2, length, length), F32),
            pltpu.VMEM((length, length), F32),
            pltpu.VMEM((4, length, length), BF16),
            pltpu.VMEM((2, 3, 2, rows_all, tile), BF16),
            packs, packs,
            wide, wide, wide, wide, wide, wide,
            pltpu.VMEM((2, length, length), F32),
            pltpu.VMEM((2 * length, length), BF16),
            pltpu.VMEM((length, 2 * length), BF16),
            pltpu.VMEM((2, length, length), F32),
            pltpu.VMEM((2, length, length), F32),
            pltpu.VMEM((2, 2, 2, rows_all, tile), BF16),
            pltpu.VMEM((2, 2, rows_all, tile), F32),
            packs,
            pltpu.VMEM((2, 2, 2, rows_all, tile), BF16),
            packs, packs,
            pltpu.VMEM((2, 2, tile, tile), F32),
            pltpu.VMEM((2, 2, 2, tile, tile), BF16),
            pltpu.VMEM((2, 2, 2, tile // 2, tile), BF16),
            pltpu.SemaphoreType.DMA((4, 2, 4)),
            pltpu.SemaphoreType.DMA((4, 2, 4)),
            pltpu.SemaphoreType.DMA((5,)),
        ],
        compiler_params=pltpu.CompilerParams(
            collective_id=0, has_side_effects=True, vmem_limit_bytes=63 * 1024 * 1024
        ),
    )(
        offsets, owned, object_slices, probe,
        measured, tables,
    )


def solution(mesh):
    in_specs = (
        P(None, None, ("groups", "row"), "col"),
        P(),
        P(("groups", "row"), "col", None, None, None),
        P(("groups", "row"), "col", None, None),
        P(("groups", "row"), "col"),
    )
    out_specs = P(None, None, ("groups", "row"), "col")
    body = functools.partial(shards, mesh.shape["row"], mesh.shape["col"])
    return jax.shard_map(body, mesh=mesh, in_specs=in_specs, out_specs=out_specs, check_vma=False)
```

```python
import functools
import math

import jax
import jax.numpy as jnp
import numpy as np
from jax import lax
from jax.experimental import pallas as pl
from jax.experimental.pallas import tpu as pltpu
from jax.sharding import PartitionSpec as P

MESH = pl.DeviceIdType.MESH
F32 = jnp.float32
BF16 = jnp.bfloat16
STEPS = (-2, -1, 1, 2)


def make_tables(length):
    counter = np.arange(length, dtype=np.int32)
    differ = (counter[:, None] - counter[None, :]) % length
    chirp = (differ * differ % (2 * length)).astype(np.float32) * np.float32(math.pi / length)
    product = counter[:, None] * counter[None, :] % length
    fourier = product.astype(np.float32) * np.float32(-2.0 * math.pi / length)
    scaling = np.float32(1.0 / math.sqrt(length))
    parts = (np.cos(chirp), np.sin(chirp), np.cos(fourier), np.sin(fourier))
    return jnp.asarray(np.stack(parts) * scaling, BF16)


def kernel(
    n_row, n_col, tile, length,
    offs_ref, owned_ref, obj_ref, probe_hbm, meas_hbm, tables_hbm,
    out_ref,
    probe_ref, meas_ref, tables_ref, own_top, peer_top, strip, side_send, sides, recv_pack, send_pack, chirp_w, chirp_c, left_f, left_b, right_f, right_b,
    prolled, stacked, halves, phi, second, gsend, gown, gpack, crecv, cpack, dsend, down, drecv,
    dhalf, send_sem, recv_sem, load_sem,
):
    row = lax.axis_index("row")
    col = lax.axis_index("col")
    half = tile // 2
    n = length
    rows_all = 4 * tile
    spot = {"row": (row, n_row), "col": (col, n_col)}

    def has(axis, step):
        at, count = spot[axis]
        return jnp.logical_and(at + step >= 0, at + step < count)

    loads = [
        pltpu.make_async_copy(src, dst, load_sem.at[k])
        for k, (src, dst) in enumerate((
            (obj_ref.at[0], strip.at[0, :, tile:2 * tile]),
            (obj_ref.at[1], strip.at[1, :, tile:2 * tile]),
            (probe_hbm, probe_ref),
            (tables_hbm, tables_ref),
            (meas_hbm.at[0, 0, 0], meas_ref),
        ))
    ]
    for load in loads:
        load.start()

    barrier = pltpu.get_barrier_semaphore()
    peers = jnp.int32(0)
    for axis in ("row", "col"):
        for step in STEPS:
            there = has(axis, step)
            peers = peers + there.astype(jnp.int32)

            @pl.when(there)
            def _(axis=axis, step=step):
                pl.semaphore_signal(
                    barrier, inc=1, device_id={axis: spot[axis][0] + step}, device_id_type=MESH
                )

    pl.semaphore_wait(barrier, peers)

    def endpoints(phase, s):
        if phase == 0:
            ends = (
                (obj_ref.at[s, :, 0:half], strip.at[s, :, 3 * tile:3 * tile + half]),
                (obj_ref.at[s], strip.at[s, :, 2 * tile:3 * tile]),
                (obj_ref.at[s], strip.at[s, :, 0:tile]),
                (obj_ref.at[s, :, half:tile], strip.at[s, :, 3 * tile + half:4 * tile]),
            )
        elif phase == 1:
            ends = (
                (send_pack.at[s, 1], recv_pack.at[s, 0]),
                (side_send.at[s, 0], sides.at[s, 1]),
                (side_send.at[s, 1], sides.at[s, 0]),
                (send_pack.at[s, 0], recv_pack.at[s, 1]),
            )
        elif phase == 2:
            ends = (
                (gpack.at[s, 1], cpack.at[s, 1]),
                (gsend.at[s, 0], crecv.at[s, 0]),
                (gsend.at[s, 1], crecv.at[s, 1]),
                (gpack.at[s, 0], cpack.at[s, 0]),
            )
        elif phase == 4:
            ends = tuple((own_top, peer_top.at[3 - k]) for k in range(4))
        else:
            ends = (
                (dsend.at[s, :, 3 * tile + half:4 * tile], dhalf.at[s, 1]),
                (dsend.at[s, :, 0:tile], drecv.at[s, 0]),
                (dsend.at[s, :, 2 * tile:3 * tile], drecv.at[s, 1]),
                (dsend.at[s, :, 3 * tile:3 * tile + half], dhalf.at[s, 0]),
            )
        return "col" if phase in (1, 2, 4) else "row", ends

    def descriptors(phase, s, steps=STEPS):
        axis, ends = endpoints(phase, s)
        made = {}
        for step in steps:
            k = STEPS.index(step)
            made[step] = (
                pltpu.make_async_remote_copy(
                    src_ref=ends[k][0],
                    dst_ref=ends[k][1],
                    send_sem=send_sem.at[phase, s, k],
                    recv_sem=recv_sem.at[phase, s, k],
                    device_id={axis: spot[axis][0] + step},
                    device_id_type=MESH,
                )
            )
        return axis, made

    def start(phase, s, steps=(-2, 2, -1, 1)):
        axis, made = descriptors(phase, s, steps)
        for step in steps:
            copy = made[step]

            @pl.when(has(axis, step))
            def _(copy=copy):
                copy.start()

    def wait_recv(phase, s):
        axis, made = descriptors(phase, s)
        for k, step in enumerate(STEPS):
            @pl.when(has(axis, -step))
            def _(copy=made[step]):
                copy.wait_recv()

    def wait_send(phase, s):
        axis, made = descriptors(phase, s)
        for step, copy in made.items():
            @pl.when(has(axis, step))
            def _(copy=copy):
                copy.wait_send()

    def clear(phase, s):
        axis, ends = endpoints(phase, s)
        for k, step in enumerate(STEPS):
            @pl.when(jnp.logical_not(has(axis, -step)))
            def _(target=ends[k][1]):
                target[...] = jnp.zeros(target.shape, target.dtype)

    start(0, 0)
    u = offs_ref[0, 0, 0, 0]
    v = offs_ref[0, 0, 0, 1]
    own_top[...] = jnp.full(own_top.shape, u.astype(F32))
    start(4, 0)
    clear(4, 0)
    for phase in range(2):
        for s in range(2):
            clear(phase, s)
    shift_u = lax.rem(u + n - half, n)
    shift_v = lax.rem(v + n - half, n)

    def pack(re, im, left):
        lane = lax.broadcasted_iota(jnp.int32, re.shape, 1)
        moved = pltpu.roll(im, half, 1)
        return jnp.where(lane < half, re, moved) if left else jnp.where(lane < half, moved, re)

    def unpack(packed):
        return packed, pltpu.roll(packed, half, 1)

    row_half = lax.broadcasted_iota(jnp.int32, (half, tile), 0).astype(F32)

    def row_masks(top):
        return row_half >= top - half, row_half < top

    def pick_rows(x, masks):
        top = jnp.where(masks[0], x[0:half], x[n:n + half])
        bottom = jnp.where(masks[1], x[n - half:n], x[n + half:n + tile])
        return jnp.concatenate([top, x[half:n - half], bottom], axis=0)

    def spread_rows(x, masks):
        top, bottom = x[0:half], x[n - half:n]
        zero = jnp.zeros_like(top)
        return jnp.concatenate(
            [
                jnp.where(masks[0], top, zero), x[half:n - half], jnp.where(masks[1], bottom, zero),
                jnp.where(masks[0], zero, top), jnp.where(masks[1], zero, bottom),
            ],
            axis=0,
        )

    def second_phase(s, peer_masks):
        loads[s].wait()
        wait_recv(0, s)
        re = strip[s, 0].astype(F32)
        im = strip[s, 1].astype(F32)
        packed = {2: (pack(re, im, False), 0), -2: (pack(re, im, True), 1)}
        for step in (2, -2):
            send_pack[s, packed[step][1]] = pick_rows(packed[step][0], peer_masks[step]).astype(BF16)
            start(1, s, (step,))
        for side, step in enumerate((-1, 1)):
            side_send[s, side, 0] = pick_rows(re, peer_masks[step]).astype(BF16)
            side_send[s, side, 1] = pick_rows(im, peer_masks[step]).astype(BF16)
            start(1, s, (step,))

    def fill(target, a, b, c, d):
        target[0:n, 0:n] = a
        target[0:n, n:2 * n] = b
        target[n:2 * n, 0:n] = c
        target[n:2 * n, n:2 * n] = d

    loads[2].wait()
    for k in range(2):
        prolled[k] = pltpu.roll(pltpu.roll(probe_ref[k], shift_u, 0), shift_v, 1)
    own_masks = row_masks(own_top[0:1])
    wait_recv(4, 0)
    peer_masks = {step: row_masks(peer_top[k, 0:1]) for k, step in enumerate(STEPS)}
    second_phase(0, peer_masks)
    start(0, 1)
    loads[3].wait()
    hre, him = tables_ref[0], tables_ref[1]
    fill(chirp_w, hre, him, -him, hre)
    fill(chirp_c, hre, -him, him, hre)
    for phase in range(2, 4):
        for s in range(2):
            clear(phase, s)
    fre, fim = tables_ref[2].astype(F32), tables_ref[3].astype(F32)

    def rolled(shift, axis):
        return pltpu.roll(fre, shift, axis).astype(BF16), pltpu.roll(fim, shift, axis).astype(BF16)

    re, im = rolled(shift_u, 1)
    fill(left_f, re, -im, im, re)
    re, im = rolled(shift_u, 0)
    fill(left_b, re, im, -im, re)
    re, im = rolled(shift_v, 0)
    fill(right_f, re, im, -im, re)
    re, im = rolled(shift_v, 1)
    fill(right_b, re, -im, im, re)

    lane_full = lax.broadcasted_iota(jnp.int32, (n, tile), 1)
    near_left = lane_full >= v - half
    near_right = lane_full + 2 * tile < v + n - half

    def window(s):
        left_alt = unpack(recv_pack[s, 0].astype(F32))
        right_alt = unpack(recv_pack[s, 1].astype(F32))
        made = []
        for k in range(2):
            made.append((
                jnp.where(near_left, sides[s, 0, k].astype(F32), left_alt[k]),
                pick_rows(strip[s, k].astype(F32), own_masks),
                jnp.where(near_right, sides[s, 1, k].astype(F32), right_alt[k]),
            ))
        return made

    def left_mul(table):
        product = jnp.dot(table[...], stacked[...], preferred_element_type=F32)
        halves[:, 0:n] = product[0:n].astype(BF16)
        halves[:, n:2 * n] = product[n:2 * n].astype(BF16)

    def right_mul(table, k):
        columns = [table[:, at:at + tile] for at in (k * tile, n + k * tile)]
        product = jnp.dot(
            halves[...], jnp.concatenate(columns, axis=1), preferred_element_type=F32
        )
        return product[:, 0:tile], product[:, tile:2 * tile]

    def scatter_slot(s, k, grad_re, grad_im):
        if k == 1:
            gown[s, 0], gown[s, 1] = grad_re, grad_im
            return
        near = near_left if k == 0 else near_right
        zero = jnp.zeros_like(grad_re)
        far = [jnp.where(near, zero, grad) for grad in (grad_re, grad_im)]
        gpack[s, k // 2] = pack(far[0], far[1], k == 0).astype(BF16)
        for part, grad in enumerate((grad_re, grad_im)):
            gsend[s, k // 2, part] = jnp.where(near, grad, zero).astype(BF16)
        start(2, s, (2, -1) if k == 0 else (-2, 1))

    def scatter_rows(s):
        wait_recv(2, s)
        lane = lax.broadcasted_iota(jnp.int32, (rows_all, tile), 1)
        lefts = unpack(spread_rows(cpack[s, 0].astype(F32), peer_masks[-2]))
        rights = unpack(spread_rows(cpack[s, 1].astype(F32), peer_masks[2]))
        for k in range(2):
            total = spread_rows(gown[s, k], own_masks)
            total = total + spread_rows(crecv[s, 0, k].astype(F32), peer_masks[1])
            total = total + spread_rows(crecv[s, 1, k].astype(F32), peer_masks[-1])
            total = total + jnp.where(lane < half, lefts[k], rights[k])
            dsend[s, k] = total.astype(BF16)
            down[s, k] = total[tile:2 * tile]
        start(3, s)

    def finish(s):
        wait_recv(3, s)
        keep = owned_ref[0, 0].astype(F32)
        for k in range(2):
            total = down[s, k] + drecv[s, 0, k].astype(F32) + drecv[s, 1, k].astype(F32)
            ends = jnp.concatenate([dhalf[s, 0, k], dhalf[s, 1, k]], axis=0).astype(F32)
            out_ref[s, k] = (total + ends) * keep

    def lanes_of(k):
        return slice(k * tile, (k + 1) * tile)

    def stack(k, re, im):
        stacked[0:n, lanes_of(k)] = re.astype(BF16)
        stacked[n:2 * n, lanes_of(k)] = im.astype(BF16)

    wait_recv(1, 0)
    second_phase(1, peer_masks)
    first_re, first_im = window(0)
    for k in range(3):
        p, q = prolled[0, :, lanes_of(k)], prolled[1, :, lanes_of(k)]
        a, b = first_re[k], first_im[k]
        stack(k, p * a - q * b, p * b + q * a)
    left_mul(chirp_c)
    for k in range(3):
        phi[0, :, lanes_of(k)], phi[1, :, lanes_of(k)] = right_mul(chirp_w, k)
    wait_recv(1, 1)
    second_re, second_im = window(1)
    for k in range(3):
        a, b = second_re[k], second_im[k]
        second[0, :, lanes_of(k)], second[1, :, lanes_of(k)] = a, b
        p, q = phi[0, :, lanes_of(k)], phi[1, :, lanes_of(k)]
        stack(k, p * a - q * b, p * b + q * a)
    left_mul(left_f)
    loads[4].wait()
    for k in range(3):
        wave_re, wave_im = right_mul(right_f, k)
        power = wave_re * wave_re + wave_im * wave_im
        ratio = meas_ref[:, lanes_of(k)] * lax.rsqrt(jnp.maximum(power, 0.25))
        stack(k, wave_re - ratio * wave_re, wave_im - ratio * wave_im)
    left_mul(left_b)
    for k in (0, 2, 1):
        back_re, back_im = right_mul(right_b, k)
        p, q = phi[0, :, lanes_of(k)], phi[1, :, lanes_of(k)]
        scatter_slot(1, k, p * back_re + q * back_im, p * back_im - q * back_re)
        a, b = second[0, :, lanes_of(k)], second[1, :, lanes_of(k)]
        stack(k, a * back_re + b * back_im, a * back_im - b * back_re)
    left_mul(chirp_w)
    for k in (0, 2, 1):
        front_re, front_im = right_mul(chirp_c, k)
        p, q = prolled[0, :, lanes_of(k)], prolled[1, :, lanes_of(k)]
        scatter_slot(0, k, p * front_re + q * front_im, p * front_im - q * front_re)
    scatter_rows(1)
    scatter_rows(0)
    finish(1)
    finish(0)
    for phase in range(4):
        for s in range(2):
            wait_send(phase, s)
    wait_send(4, 0)


def shards(n_row, n_col, object_slices, probe, measured, offsets, owned):
    tile = object_slices.shape[2]
    length = probe.shape[1]
    tables = make_tables(length)
    rows_all = 4 * tile
    vmem = pl.BlockSpec(memory_space=pltpu.VMEM)
    hbm = pl.BlockSpec(memory_space=pltpu.HBM)
    smem = pl.BlockSpec(memory_space=pltpu.SMEM)
    wide = pltpu.VMEM((2 * length, 2 * length), BF16)
    packs = pltpu.VMEM((2, 2, length, tile), BF16)
    sides = pltpu.VMEM((2, 2, 2, length, tile), BF16)
    return pl.pallas_call(
        functools.partial(kernel, n_row, n_col, tile, length),
        out_shape=jax.ShapeDtypeStruct(object_slices.shape, F32),
        in_specs=[smem, smem] + [hbm] * 4,
        out_specs=vmem,
        scratch_shapes=[
            pltpu.VMEM((2, length, length), F32),
            pltpu.VMEM((length, length), F32),
            pltpu.VMEM((4, length, length), BF16),
            pltpu.VMEM((8, tile), F32),
            pltpu.VMEM((4, 8, tile), F32),
            pltpu.VMEM((2, 2, rows_all, tile), BF16),
            sides, sides, packs, packs,
            wide, wide, wide, wide, wide, wide,
            pltpu.VMEM((2, length, length), F32),
            pltpu.VMEM((2 * length, length), BF16),
            pltpu.VMEM((length, 2 * length), BF16),
            pltpu.VMEM((2, length, length), F32),
            pltpu.VMEM((2, length, length), F32),
            sides,
            pltpu.VMEM((2, 2, length, tile), F32),
            packs, sides, packs,
            pltpu.VMEM((2, 2, rows_all, tile), BF16),
            pltpu.VMEM((2, 2, tile, tile), F32),
            pltpu.VMEM((2, 2, 2, tile, tile), BF16),
            pltpu.VMEM((2, 2, 2, tile // 2, tile), BF16),
            pltpu.SemaphoreType.DMA((5, 2, 4)),
            pltpu.SemaphoreType.DMA((5, 2, 4)),
            pltpu.SemaphoreType.DMA((5,)),
        ],
        compiler_params=pltpu.CompilerParams(
            collective_id=0, has_side_effects=True, vmem_limit_bytes=63 * 1024 * 1024
        ),
    )(
        offsets, owned, object_slices, probe,
        measured, tables,
    )


def solution(mesh):
    in_specs = (
        P(None, None, ("groups", "row"), "col"),
        P(),
        P(("groups", "row"), "col", None, None, None),
        P(("groups", "row"), "col", None, None),
        P(("groups", "row"), "col"),
    )
    out_specs = P(None, None, ("groups", "row"), "col")
    body = functools.partial(shards, mesh.shape["row"], mesh.shape["col"])
    return jax.shard_map(body, mesh=mesh, in_specs=in_specs, out_specs=out_specs, check_vma=False)
```

```python
import functools
import math

import jax
import jax.numpy as jnp
import numpy as np
from jax import lax
from jax.experimental import pallas as pl
from jax.experimental.pallas import tpu as pltpu
from jax.sharding import PartitionSpec as P

MESH = pl.DeviceIdType.MESH
F32 = jnp.float32
BF16 = jnp.bfloat16
STEPS = (-2, -1, 1, 2)


def make_tables(length):
    counter = np.arange(length, dtype=np.int32)
    differ = (counter[:, None] - counter[None, :]) % length
    chirp = (differ * differ % (2 * length)).astype(np.float32) * np.float32(math.pi / length)
    product = counter[:, None] * counter[None, :] % length
    fourier = product.astype(np.float32) * np.float32(-2.0 * math.pi / length)
    scaling = np.float32(1.0 / math.sqrt(length))
    parts = (np.cos(chirp), np.sin(chirp), np.cos(fourier), np.sin(fourier))
    return jnp.asarray(np.stack(parts) * scaling, BF16)


def kernel(
    n_row, n_col, tile, length,
    offs_ref, owned_ref, obj_ref, probe_hbm, meas_hbm, tables_hbm,
    out_ref,
    probe_ref, meas_ref, tables_ref, own_top, peer_top, strip, side_send, sides, recv_pack, send_pack, chirp_w, chirp_c, left_f, left_b, right_f, right_b,
    prolled, stacked, halves, phi, second, gsend, gown, gpack, crecv, cpack, dsend, down, drecv,
    dhalf, send_sem, recv_sem, load_sem,
):
    row = lax.axis_index("row")
    col = lax.axis_index("col")
    half = tile // 2
    n = length
    rows_all = 4 * tile
    spot = {"row": (row, n_row), "col": (col, n_col)}

    def has(axis, step):
        at, count = spot[axis]
        return jnp.logical_and(at + step >= 0, at + step < count)

    loads = [
        pltpu.make_async_copy(src, dst, load_sem.at[k])
        for k, (src, dst) in enumerate((
            (obj_ref.at[0], strip.at[0, :, tile:2 * tile]),
            (obj_ref.at[1], strip.at[1, :, tile:2 * tile]),
            (probe_hbm, probe_ref),
            (tables_hbm, tables_ref),
            (meas_hbm.at[0, 0, 0], meas_ref),
        ))
    ]
    for load in loads:
        load.start()

    barrier = pltpu.get_barrier_semaphore()
    peers = jnp.int32(0)
    for axis in ("row", "col"):
        for step in STEPS:
            there = has(axis, step)
            peers = peers + there.astype(jnp.int32)

            @pl.when(there)
            def _(axis=axis, step=step):
                pl.semaphore_signal(
                    barrier, inc=1, device_id={axis: spot[axis][0] + step}, device_id_type=MESH
                )

    pl.semaphore_wait(barrier, peers)

    def endpoints(phase, s):
        if phase == 0:
            ends = (
                (obj_ref.at[s, :, 0:half], strip.at[s, :, 3 * tile:3 * tile + half]),
                (obj_ref.at[s], strip.at[s, :, 2 * tile:3 * tile]),
                (obj_ref.at[s], strip.at[s, :, 0:tile]),
                (obj_ref.at[s, :, half:tile], strip.at[s, :, 3 * tile + half:4 * tile]),
            )
        elif phase == 1:
            ends = (
                (send_pack.at[s, 1], recv_pack.at[s, 0]),
                (side_send.at[s, 0], sides.at[s, 1]),
                (side_send.at[s, 1], sides.at[s, 0]),
                (send_pack.at[s, 0], recv_pack.at[s, 1]),
            )
        elif phase == 2:
            ends = (
                (gpack.at[s, 1], cpack.at[s, 1]),
                (gsend.at[s, 0], crecv.at[s, 0]),
                (gsend.at[s, 1], crecv.at[s, 1]),
                (gpack.at[s, 0], cpack.at[s, 0]),
            )
        elif phase == 4:
            ends = tuple((own_top, peer_top.at[3 - k]) for k in range(4))
        else:
            ends = (
                (dsend.at[s, :, 3 * tile + half:4 * tile], dhalf.at[s, 1]),
                (dsend.at[s, :, 0:tile], drecv.at[s, 0]),
                (dsend.at[s, :, 2 * tile:3 * tile], drecv.at[s, 1]),
                (dsend.at[s, :, 3 * tile:3 * tile + half], dhalf.at[s, 0]),
            )
        return "col" if phase in (1, 2, 4) else "row", ends

    def descriptors(phase, s, steps=STEPS):
        axis, ends = endpoints(phase, s)
        made = {}
        for step in steps:
            k = STEPS.index(step)
            made[step] = (
                pltpu.make_async_remote_copy(
                    src_ref=ends[k][0],
                    dst_ref=ends[k][1],
                    send_sem=send_sem.at[phase, s, k],
                    recv_sem=recv_sem.at[phase, s, k],
                    device_id={axis: spot[axis][0] + step},
                    device_id_type=MESH,
                )
            )
        return axis, made

    def start(phase, s, steps=(-2, 2, -1, 1)):
        axis, made = descriptors(phase, s, steps)
        for step in steps:
            copy = made[step]

            @pl.when(has(axis, step))
            def _(copy=copy):
                copy.start()

    def wait_recv(phase, s):
        axis, made = descriptors(phase, s)
        for k, step in enumerate(STEPS):
            @pl.when(has(axis, -step))
            def _(copy=made[step]):
                copy.wait_recv()

    def wait_send(phase, s):
        axis, made = descriptors(phase, s)
        for step, copy in made.items():
            @pl.when(has(axis, step))
            def _(copy=copy):
                copy.wait_send()

    def clear(phase, s):
        axis, ends = endpoints(phase, s)
        for k, step in enumerate(STEPS):
            @pl.when(jnp.logical_not(has(axis, -step)))
            def _(target=ends[k][1]):
                target[...] = jnp.zeros(target.shape, target.dtype)

    start(0, 0)
    u = offs_ref[0, 0, 0, 0]
    v = offs_ref[0, 0, 0, 1]
    own_top[...] = jnp.full(own_top.shape, u.astype(F32))
    start(4, 0)
    clear(4, 0)
    for phase in range(2):
        for s in range(2):
            clear(phase, s)
    shift_u = lax.rem(u + n - half, n)
    shift_v = lax.rem(v + n - half, n)

    def pack(re, im, left):
        lane = lax.broadcasted_iota(jnp.int32, re.shape, 1)
        moved = pltpu.roll(im, half, 1)
        return jnp.where(lane < half, re, moved) if left else jnp.where(lane < half, moved, re)

    def unpack(packed):
        return packed, pltpu.roll(packed, half, 1)

    row_half = lax.broadcasted_iota(jnp.int32, (half, tile), 0).astype(F32)

    def row_masks(top):
        return row_half >= top - half, row_half < top

    def pick_rows(x, masks):
        top = jnp.where(masks[0], x[0:half], x[n:n + half])
        bottom = jnp.where(masks[1], x[n - half:n], x[n + half:n + tile])
        return jnp.concatenate([top, x[half:n - half], bottom], axis=0)

    def spread_rows(x, masks):
        top, bottom = x[0:half], x[n - half:n]
        zero = jnp.zeros_like(top)
        return jnp.concatenate(
            [
                jnp.where(masks[0], top, zero), x[half:n - half], jnp.where(masks[1], bottom, zero),
                jnp.where(masks[0], zero, top), jnp.where(masks[1], zero, bottom),
            ],
            axis=0,
        )

    def second_phase(s, peer_masks):
        loads[s].wait()
        wait_recv(0, s)
        re = strip[s, 0].astype(F32)
        im = strip[s, 1].astype(F32)
        packed = {2: (pack(re, im, False), 0), -2: (pack(re, im, True), 1)}
        for step in (2, -2):
            send_pack[s, packed[step][1]] = pick_rows(packed[step][0], peer_masks[step]).astype(BF16)
            start(1, s, (step,))
        for side, step in enumerate((-1, 1)):
            side_send[s, side, 0] = pick_rows(re, peer_masks[step]).astype(BF16)
            side_send[s, side, 1] = pick_rows(im, peer_masks[step]).astype(BF16)
            start(1, s, (step,))

    def fill(target, a, b, c, d):
        target[0:n, 0:n] = a
        target[0:n, n:2 * n] = b
        target[n:2 * n, 0:n] = c
        target[n:2 * n, n:2 * n] = d

    loads[2].wait()
    for k in range(2):
        prolled[k] = pltpu.roll(pltpu.roll(probe_ref[k], shift_u, 0), shift_v, 1)
    own_masks = row_masks(own_top[0:1])
    wait_recv(4, 0)
    peer_masks = {step: row_masks(peer_top[k, 0:1]) for k, step in enumerate(STEPS)}
    second_phase(0, peer_masks)
    start(0, 1)
    loads[3].wait()
    hre, him = tables_ref[0], tables_ref[1]
    fill(chirp_w, hre, him, -him, hre)
    fill(chirp_c, hre, -him, him, hre)
    for phase in range(2, 4):
        for s in range(2):
            clear(phase, s)
    fre, fim = tables_ref[2].astype(F32), tables_ref[3].astype(F32)

    def rolled(shift, axis):
        return pltpu.roll(fre, shift, axis).astype(BF16), pltpu.roll(fim, shift, axis).astype(BF16)

    re, im = rolled(shift_u, 1)
    fill(left_f, re, -im, im, re)
    re, im = rolled(shift_u, 0)
    fill(left_b, re, im, -im, re)
    re, im = rolled(shift_v, 0)
    fill(right_f, re, im, -im, re)
    re, im = rolled(shift_v, 1)
    fill(right_b, re, -im, im, re)

    lane_full = lax.broadcasted_iota(jnp.int32, (n, tile), 1)
    near_left = lane_full >= v - half
    near_right = lane_full + 2 * tile < v + n - half

    def window(s):
        left_alt = unpack(recv_pack[s, 0].astype(F32))
        right_alt = unpack(recv_pack[s, 1].astype(F32))
        made = []
        for k in range(2):
            made.append((
                jnp.where(near_left, sides[s, 0, k].astype(F32), left_alt[k]),
                pick_rows(strip[s, k].astype(F32), own_masks),
                jnp.where(near_right, sides[s, 1, k].astype(F32), right_alt[k]),
            ))
        return made

    def left_mul(table):
        product = jnp.dot(table[...], stacked[...], preferred_element_type=F32)
        halves[:, 0:n] = product[0:n].astype(BF16)
        halves[:, n:2 * n] = product[n:2 * n].astype(BF16)

    def right_mul(table, k):
        columns = [table[:, at:at + tile] for at in (k * tile, n + k * tile)]
        product = jnp.dot(
            halves[...], jnp.concatenate(columns, axis=1), preferred_element_type=F32
        )
        return product[:, 0:tile], product[:, tile:2 * tile]

    def scatter_slot(s, k, grad_re, grad_im):
        if k == 1:
            gown[s, 0], gown[s, 1] = grad_re, grad_im
            return
        near = near_left if k == 0 else near_right
        zero = jnp.zeros_like(grad_re)
        far = [jnp.where(near, zero, grad) for grad in (grad_re, grad_im)]
        gpack[s, k // 2] = pack(far[0], far[1], k == 0).astype(BF16)
        for part, grad in enumerate((grad_re, grad_im)):
            gsend[s, k // 2, part] = jnp.where(near, grad, zero).astype(BF16)
        start(2, s, (2, -1) if k == 0 else (-2, 1))

    def scatter_rows(s):
        wait_recv(2, s)
        lane = lax.broadcasted_iota(jnp.int32, (rows_all, tile), 1)
        lefts = unpack(spread_rows(cpack[s, 0].astype(F32), peer_masks[-2]))
        rights = unpack(spread_rows(cpack[s, 1].astype(F32), peer_masks[2]))
        for k in range(2):
            total = spread_rows(gown[s, k], own_masks)
            total = total + spread_rows(crecv[s, 0, k].astype(F32), peer_masks[1])
            total = total + spread_rows(crecv[s, 1, k].astype(F32), peer_masks[-1])
            total = total + jnp.where(lane < half, lefts[k], rights[k])
            dsend[s, k] = total.astype(BF16)
            down[s, k] = total[tile:2 * tile]
        start(3, s)

    def finish(s):
        wait_recv(3, s)
        keep = owned_ref[0, 0].astype(F32)
        for k in range(2):
            total = down[s, k] + drecv[s, 0, k].astype(F32) + drecv[s, 1, k].astype(F32)
            ends = jnp.concatenate([dhalf[s, 0, k], dhalf[s, 1, k]], axis=0).astype(F32)
            out_ref[s, k] = (total + ends) * keep

    def lanes_of(k):
        return slice(k * tile, (k + 1) * tile)

    def stack(k, re, im):
        stacked[0:n, lanes_of(k)] = re.astype(BF16)
        stacked[n:2 * n, lanes_of(k)] = im.astype(BF16)

    second_phase(1, peer_masks)
    wait_recv(1, 0)
    first_re, first_im = window(0)
    for k in range(3):
        p, q = prolled[0, :, lanes_of(k)], prolled[1, :, lanes_of(k)]
        a, b = first_re[k], first_im[k]
        stack(k, p * a - q * b, p * b + q * a)
    left_mul(chirp_c)
    for k in range(3):
        phi[0, :, lanes_of(k)], phi[1, :, lanes_of(k)] = right_mul(chirp_w, k)
    wait_recv(1, 1)
    second_re, second_im = window(1)
    for k in range(3):
        a, b = second_re[k], second_im[k]
        second[0, :, lanes_of(k)], second[1, :, lanes_of(k)] = a, b
        p, q = phi[0, :, lanes_of(k)], phi[1, :, lanes_of(k)]
        stack(k, p * a - q * b, p * b + q * a)
    left_mul(left_f)
    loads[4].wait()
    for k in range(3):
        wave_re, wave_im = right_mul(right_f, k)
        power = wave_re * wave_re + wave_im * wave_im
        ratio = meas_ref[:, lanes_of(k)] * lax.rsqrt(jnp.maximum(power, 0.25))
        stack(k, wave_re - ratio * wave_re, wave_im - ratio * wave_im)
    left_mul(left_b)
    for k in (0, 2, 1):
        back_re, back_im = right_mul(right_b, k)
        p, q = phi[0, :, lanes_of(k)], phi[1, :, lanes_of(k)]
        scatter_slot(1, k, p * back_re + q * back_im, p * back_im - q * back_re)
        a, b = second[0, :, lanes_of(k)], second[1, :, lanes_of(k)]
        stack(k, a * back_re + b * back_im, a * back_im - b * back_re)
    left_mul(chirp_w)
    for k in (0, 2, 1):
        front_re, front_im = right_mul(chirp_c, k)
        p, q = prolled[0, :, lanes_of(k)], prolled[1, :, lanes_of(k)]
        scatter_slot(0, k, p * front_re + q * front_im, p * front_im - q * front_re)
    scatter_rows(1)
    scatter_rows(0)
    finish(1)
    finish(0)
    for phase in range(4):
        for s in range(2):
            wait_send(phase, s)
    wait_send(4, 0)


def shards(n_row, n_col, object_slices, probe, measured, offsets, owned):
    tile = object_slices.shape[2]
    length = probe.shape[1]
    tables = make_tables(length)
    rows_all = 4 * tile
    vmem = pl.BlockSpec(memory_space=pltpu.VMEM)
    hbm = pl.BlockSpec(memory_space=pltpu.HBM)
    smem = pl.BlockSpec(memory_space=pltpu.SMEM)
    wide = pltpu.VMEM((2 * length, 2 * length), BF16)
    packs = pltpu.VMEM((2, 2, length, tile), BF16)
    sides = pltpu.VMEM((2, 2, 2, length, tile), BF16)
    return pl.pallas_call(
        functools.partial(kernel, n_row, n_col, tile, length),
        out_shape=jax.ShapeDtypeStruct(object_slices.shape, F32),
        in_specs=[smem, smem] + [hbm] * 4,
        out_specs=vmem,
        scratch_shapes=[
            pltpu.VMEM((2, length, length), F32),
            pltpu.VMEM((length, length), F32),
            pltpu.VMEM((4, length, length), BF16),
            pltpu.VMEM((8, tile), F32),
            pltpu.VMEM((4, 8, tile), F32),
            pltpu.VMEM((2, 2, rows_all, tile), BF16),
            sides, sides, packs, packs,
            wide, wide, wide, wide, wide, wide,
            pltpu.VMEM((2, length, length), F32),
            pltpu.VMEM((2 * length, length), BF16),
            pltpu.VMEM((length, 2 * length), BF16),
            pltpu.VMEM((2, length, length), F32),
            pltpu.VMEM((2, length, length), F32),
            sides,
            pltpu.VMEM((2, 2, length, tile), F32),
            packs, sides, packs,
            pltpu.VMEM((2, 2, rows_all, tile), BF16),
            pltpu.VMEM((2, 2, tile, tile), F32),
            pltpu.VMEM((2, 2, 2, tile, tile), BF16),
            pltpu.VMEM((2, 2, 2, tile // 2, tile), BF16),
            pltpu.SemaphoreType.DMA((5, 2, 4)),
            pltpu.SemaphoreType.DMA((5, 2, 4)),
            pltpu.SemaphoreType.DMA((5,)),
        ],
        compiler_params=pltpu.CompilerParams(
            collective_id=0, has_side_effects=True, vmem_limit_bytes=63 * 1024 * 1024
        ),
    )(
        offsets, owned, object_slices, probe,
        measured, tables,
    )


def solution(mesh):
    in_specs = (
        P(None, None, ("groups", "row"), "col"),
        P(),
        P(("groups", "row"), "col", None, None, None),
        P(("groups", "row"), "col", None, None),
        P(("groups", "row"), "col"),
    )
    out_specs = P(None, None, ("groups", "row"), "col")
    body = functools.partial(shards, mesh.shape["row"], mesh.shape["col"])
    return jax.shard_map(body, mesh=mesh, in_specs=in_specs, out_specs=out_specs, check_vma=False)
```

```python
import functools
import math

import jax
import jax.numpy as jnp
import numpy as np
from jax import lax
from jax.experimental import pallas as pl
from jax.experimental.pallas import tpu as pltpu
from jax.sharding import PartitionSpec as P

MESH = pl.DeviceIdType.MESH
F32 = jnp.float32
BF16 = jnp.bfloat16
STEPS = (-2, -1, 1, 2)


def make_tables(length):
    counter = np.arange(length, dtype=np.int32)
    differ = (counter[:, None] - counter[None, :]) % length
    chirp = (differ * differ % (2 * length)).astype(np.float32) * np.float32(math.pi / length)
    product = counter[:, None] * counter[None, :] % length
    fourier = product.astype(np.float32) * np.float32(-2.0 * math.pi / length)
    scaling = np.float32(1.0 / math.sqrt(length))
    parts = (np.cos(chirp), np.sin(chirp), np.cos(fourier), np.sin(fourier))
    return jnp.asarray(np.stack(parts) * scaling, BF16)


def kernel(
    n_row, n_col, tile, length,
    offs_ref, owned_ref, obj_ref, probe_hbm, meas_hbm, tables_hbm,
    out_ref,
    probe_ref, meas_ref, tables_ref, own_top, peer_top, strip, side_send, sides, recv_pack, send_pack, chirp_w, chirp_c, left_f, left_b, right_f, right_b,
    prolled, stacked, halves, phi, second, gsend, gown, gpack, crecv, cpack, dsend, down, drecv,
    dhalf, send_sem, recv_sem, load_sem,
):
    row = lax.axis_index("row")
    col = lax.axis_index("col")
    half = tile // 2
    n = length
    rows_all = 4 * tile
    spot = {"row": (row, n_row), "col": (col, n_col)}

    def has(axis, step):
        at, count = spot[axis]
        return jnp.logical_and(at + step >= 0, at + step < count)

    loads = [
        pltpu.make_async_copy(src, dst, load_sem.at[k])
        for k, (src, dst) in enumerate((
            (obj_ref.at[0], strip.at[0, :, tile:2 * tile]),
            (obj_ref.at[1], strip.at[1, :, tile:2 * tile]),
            (probe_hbm, probe_ref),
            (tables_hbm, tables_ref),
            (meas_hbm.at[0, 0, 0], meas_ref),
        ))
    ]
    for load in loads:
        load.start()

    barrier = pltpu.get_barrier_semaphore()
    peers = jnp.int32(0)
    for axis in ("row", "col"):
        for step in STEPS:
            there = has(axis, step)
            peers = peers + there.astype(jnp.int32)

            @pl.when(there)
            def _(axis=axis, step=step):
                pl.semaphore_signal(
                    barrier, inc=1, device_id={axis: spot[axis][0] + step}, device_id_type=MESH
                )

    pl.semaphore_wait(barrier, peers)

    def endpoints(phase, s):
        if phase == 0:
            ends = (
                (obj_ref.at[s, :, 0:half], strip.at[s, :, 3 * tile:3 * tile + half]),
                (obj_ref.at[s], strip.at[s, :, 2 * tile:3 * tile]),
                (obj_ref.at[s], strip.at[s, :, 0:tile]),
                (obj_ref.at[s, :, half:tile], strip.at[s, :, 3 * tile + half:4 * tile]),
            )
        elif phase == 1:
            ends = (
                (send_pack.at[s, 1], recv_pack.at[s, 0]),
                (side_send.at[s, 0], sides.at[s, 1]),
                (side_send.at[s, 1], sides.at[s, 0]),
                (send_pack.at[s, 0], recv_pack.at[s, 1]),
            )
        elif phase == 2:
            ends = (
                (gpack.at[s, 1], cpack.at[s, 1]),
                (gsend.at[s, 0], crecv.at[s, 0]),
                (gsend.at[s, 1], crecv.at[s, 1]),
                (gpack.at[s, 0], cpack.at[s, 0]),
            )
        elif phase == 4:
            ends = tuple((own_top, peer_top.at[3 - k]) for k in range(4))
        else:
            ends = (
                (dsend.at[s, :, 3 * tile + half:4 * tile], dhalf.at[s, 1]),
                (dsend.at[s, :, 0:tile], drecv.at[s, 0]),
                (dsend.at[s, :, 2 * tile:3 * tile], drecv.at[s, 1]),
                (dsend.at[s, :, 3 * tile:3 * tile + half], dhalf.at[s, 0]),
            )
        return "col" if phase in (1, 2, 4) else "row", ends

    def descriptors(phase, s, steps=STEPS):
        axis, ends = endpoints(phase, s)
        made = {}
        for step in steps:
            k = STEPS.index(step)
            made[step] = (
                pltpu.make_async_remote_copy(
                    src_ref=ends[k][0],
                    dst_ref=ends[k][1],
                    send_sem=send_sem.at[phase, s, k],
                    recv_sem=recv_sem.at[phase, s, k],
                    device_id={axis: spot[axis][0] + step},
                    device_id_type=MESH,
                )
            )
        return axis, made

    def start(phase, s, steps=(-2, 2, -1, 1)):
        axis, made = descriptors(phase, s, steps)
        for step in steps:
            copy = made[step]

            @pl.when(has(axis, step))
            def _(copy=copy):
                copy.start()

    def wait_recv(phase, s):
        axis, made = descriptors(phase, s)
        for k, step in enumerate(STEPS):
            @pl.when(has(axis, -step))
            def _(copy=made[step]):
                copy.wait_recv()

    def wait_send(phase, s):
        axis, made = descriptors(phase, s)
        for step, copy in made.items():
            @pl.when(has(axis, step))
            def _(copy=copy):
                copy.wait_send()

    def clear(phase, s):
        axis, ends = endpoints(phase, s)
        for k, step in enumerate(STEPS):
            @pl.when(jnp.logical_not(has(axis, -step)))
            def _(target=ends[k][1]):
                target[...] = jnp.zeros(target.shape, target.dtype)

    start(0, 0)
    u = offs_ref[0, 0, 0, 0]
    v = offs_ref[0, 0, 0, 1]
    own_top[...] = jnp.full(own_top.shape, u.astype(F32))
    start(4, 0)
    clear(4, 0)
    for phase in range(2):
        for s in range(2):
            clear(phase, s)
    shift_u = lax.rem(u + n - half, n)
    shift_v = lax.rem(v + n - half, n)

    def pack(re, im, left):
        lane = lax.broadcasted_iota(jnp.int32, re.shape, 1)
        moved = pltpu.roll(im, half, 1)
        return jnp.where(lane < half, re, moved) if left else jnp.where(lane < half, moved, re)

    def unpack(packed):
        return packed, pltpu.roll(packed, half, 1)

    row_half = lax.broadcasted_iota(jnp.int32, (half, tile), 0).astype(F32)

    def row_masks(top):
        return row_half >= top - half, row_half < top

    def pick_rows(x, masks):
        top = jnp.where(masks[0], x[0:half], x[n:n + half])
        bottom = jnp.where(masks[1], x[n - half:n], x[n + half:n + tile])
        return jnp.concatenate([top, x[half:n - half], bottom], axis=0)

    def spread_rows(x, masks):
        top, bottom = x[0:half], x[n - half:n]
        zero = jnp.zeros_like(top)
        return jnp.concatenate(
            [
                jnp.where(masks[0], top, zero), x[half:n - half], jnp.where(masks[1], bottom, zero),
                jnp.where(masks[0], zero, top), jnp.where(masks[1], zero, bottom),
            ],
            axis=0,
        )

    def second_phase(s, peer_masks):
        loads[s].wait()
        wait_recv(0, s)
        re = strip[s, 0].astype(F32)
        im = strip[s, 1].astype(F32)
        packed = {2: (pack(re, im, False), 0), -2: (pack(re, im, True), 1)}
        for step in (2, -2):
            send_pack[s, packed[step][1]] = pick_rows(packed[step][0], peer_masks[step]).astype(BF16)
            start(1, s, (step,))
        for side, step in enumerate((-1, 1)):
            side_send[s, side, 0] = pick_rows(re, peer_masks[step]).astype(BF16)
            side_send[s, side, 1] = pick_rows(im, peer_masks[step]).astype(BF16)
            start(1, s, (step,))

    def fill(target, a, b, c, d):
        target[0:n, 0:n] = a
        target[0:n, n:2 * n] = b
        target[n:2 * n, 0:n] = c
        target[n:2 * n, n:2 * n] = d

    loads[2].wait()
    for k in range(2):
        prolled[k] = pltpu.roll(pltpu.roll(probe_ref[k], shift_u, 0), shift_v, 1)
    own_masks = row_masks(own_top[0:1])
    wait_recv(4, 0)
    peer_masks = {step: row_masks(peer_top[k, 0:1]) for k, step in enumerate(STEPS)}
    second_phase(0, peer_masks)
    start(0, 1)
    loads[3].wait()
    hre, him = tables_ref[0], tables_ref[1]
    fill(chirp_w, hre, him, -him, hre)
    fill(chirp_c, hre, -him, him, hre)
    for phase in range(2, 4):
        for s in range(2):
            clear(phase, s)
    fre, fim = tables_ref[2].astype(F32), tables_ref[3].astype(F32)

    def rolled(shift, axis):
        return pltpu.roll(fre, shift, axis).astype(BF16), pltpu.roll(fim, shift, axis).astype(BF16)

    re, im = rolled(shift_u, 1)
    fill(left_f, re, -im, im, re)
    re, im = rolled(shift_u, 0)
    fill(left_b, re, im, -im, re)
    re, im = rolled(shift_v, 0)
    fill(right_f, re, im, -im, re)
    re, im = rolled(shift_v, 1)
    fill(right_b, re, -im, im, re)

    lane_full = lax.broadcasted_iota(jnp.int32, (n, tile), 1)
    near_left = lane_full >= v - half
    near_right = lane_full + 2 * tile < v + n - half

    def window(s):
        left_alt = unpack(recv_pack[s, 0].astype(F32))
        right_alt = unpack(recv_pack[s, 1].astype(F32))
        made = []
        for k in range(2):
            made.append((
                jnp.where(near_left, sides[s, 0, k].astype(F32), left_alt[k]),
                pick_rows(strip[s, k].astype(F32), own_masks),
                jnp.where(near_right, sides[s, 1, k].astype(F32), right_alt[k]),
            ))
        return made

    def left_mul(table):
        product = jnp.dot(table[...], stacked[...], preferred_element_type=F32)
        halves[:, 0:n] = product[0:n].astype(BF16)
        halves[:, n:2 * n] = product[n:2 * n].astype(BF16)

    def right_mul(table, k):
        columns = [table[:, at:at + tile] for at in (k * tile, n + k * tile)]
        product = jnp.dot(
            halves[...], jnp.concatenate(columns, axis=1), preferred_element_type=F32
        )
        return product[:, 0:tile], product[:, tile:2 * tile]

    def scatter_slot(s, k, grad_re, grad_im):
        if k == 1:
            gown[s, 0], gown[s, 1] = grad_re, grad_im
            return
        near = near_left if k == 0 else near_right
        zero = jnp.zeros_like(grad_re)
        far = [jnp.where(near, zero, grad) for grad in (grad_re, grad_im)]
        gpack[s, k // 2] = pack(far[0], far[1], k == 0).astype(BF16)
        for part, grad in enumerate((grad_re, grad_im)):
            gsend[s, k // 2, part] = jnp.where(near, grad, zero).astype(BF16)
        start(2, s, (2, -1) if k == 0 else (-2, 1))

    def scatter_rows(s):
        wait_recv(2, s)
        lane = lax.broadcasted_iota(jnp.int32, (rows_all, tile), 1)
        lefts = unpack(spread_rows(cpack[s, 0].astype(F32), peer_masks[-2]))
        rights = unpack(spread_rows(cpack[s, 1].astype(F32), peer_masks[2]))
        totals = []
        for k in range(2):
            total = spread_rows(gown[s, k], own_masks)
            total = total + spread_rows(crecv[s, 0, k].astype(F32), peer_masks[1])
            total = total + spread_rows(crecv[s, 1, k].astype(F32), peer_masks[-1])
            total = total + jnp.where(lane < half, lefts[k], rights[k])
            totals.append(total)
        for low, high, step in (
            (3 * tile, 3 * tile + half, 2), (3 * tile + half, 4 * tile, -2),
            (0, tile, -1), (2 * tile, 3 * tile, 1),
        ):
            for k in range(2):
                dsend[s, k, low:high] = totals[k][low:high].astype(BF16)
            start(3, s, (step,))
        for k in range(2):
            down[s, k] = totals[k][tile:2 * tile]

    def finish(s):
        wait_recv(3, s)
        keep = owned_ref[0, 0].astype(F32)
        for k in range(2):
            total = down[s, k] + drecv[s, 0, k].astype(F32) + drecv[s, 1, k].astype(F32)
            ends = jnp.concatenate([dhalf[s, 0, k], dhalf[s, 1, k]], axis=0).astype(F32)
            out_ref[s, k] = (total + ends) * keep

    def lanes_of(k):
        return slice(k * tile, (k + 1) * tile)

    def stack(k, re, im):
        stacked[0:n, lanes_of(k)] = re.astype(BF16)
        stacked[n:2 * n, lanes_of(k)] = im.astype(BF16)

    second_phase(1, peer_masks)
    wait_recv(1, 0)
    first_re, first_im = window(0)
    for k in range(3):
        p, q = prolled[0, :, lanes_of(k)], prolled[1, :, lanes_of(k)]
        a, b = first_re[k], first_im[k]
        stack(k, p * a - q * b, p * b + q * a)
    left_mul(chirp_c)
    for k in range(3):
        phi[0, :, lanes_of(k)], phi[1, :, lanes_of(k)] = right_mul(chirp_w, k)
    wait_recv(1, 1)
    second_re, second_im = window(1)
    for k in range(3):
        a, b = second_re[k], second_im[k]
        second[0, :, lanes_of(k)], second[1, :, lanes_of(k)] = a, b
        p, q = phi[0, :, lanes_of(k)], phi[1, :, lanes_of(k)]
        stack(k, p * a - q * b, p * b + q * a)
    left_mul(left_f)
    loads[4].wait()
    for k in range(3):
        wave_re, wave_im = right_mul(right_f, k)
        power = wave_re * wave_re + wave_im * wave_im
        ratio = meas_ref[:, lanes_of(k)] * lax.rsqrt(jnp.maximum(power, 0.25))
        stack(k, wave_re - ratio * wave_re, wave_im - ratio * wave_im)
    left_mul(left_b)
    for k in (0, 2, 1):
        back_re, back_im = right_mul(right_b, k)
        p, q = phi[0, :, lanes_of(k)], phi[1, :, lanes_of(k)]
        scatter_slot(1, k, p * back_re + q * back_im, p * back_im - q * back_re)
        a, b = second[0, :, lanes_of(k)], second[1, :, lanes_of(k)]
        stack(k, a * back_re + b * back_im, a * back_im - b * back_re)
    left_mul(chirp_w)
    for k in (0, 2, 1):
        front_re, front_im = right_mul(chirp_c, k)
        p, q = prolled[0, :, lanes_of(k)], prolled[1, :, lanes_of(k)]
        scatter_slot(0, k, p * front_re + q * front_im, p * front_im - q * front_re)
    scatter_rows(1)
    scatter_rows(0)
    finish(1)
    finish(0)
    for phase in range(4):
        for s in range(2):
            wait_send(phase, s)
    wait_send(4, 0)


def shards(n_row, n_col, object_slices, probe, measured, offsets, owned):
    tile = object_slices.shape[2]
    length = probe.shape[1]
    tables = make_tables(length)
    rows_all = 4 * tile
    vmem = pl.BlockSpec(memory_space=pltpu.VMEM)
    hbm = pl.BlockSpec(memory_space=pltpu.HBM)
    smem = pl.BlockSpec(memory_space=pltpu.SMEM)
    wide = pltpu.VMEM((2 * length, 2 * length), BF16)
    packs = pltpu.VMEM((2, 2, length, tile), BF16)
    sides = pltpu.VMEM((2, 2, 2, length, tile), BF16)
    return pl.pallas_call(
        functools.partial(kernel, n_row, n_col, tile, length),
        out_shape=jax.ShapeDtypeStruct(object_slices.shape, F32),
        in_specs=[smem, smem] + [hbm] * 4,
        out_specs=vmem,
        scratch_shapes=[
            pltpu.VMEM((2, length, length), F32),
            pltpu.VMEM((length, length), F32),
            pltpu.VMEM((4, length, length), BF16),
            pltpu.VMEM((8, tile), F32),
            pltpu.VMEM((4, 8, tile), F32),
            pltpu.VMEM((2, 2, rows_all, tile), BF16),
            sides, sides, packs, packs,
            wide, wide, wide, wide, wide, wide,
            pltpu.VMEM((2, length, length), F32),
            pltpu.VMEM((2 * length, length), BF16),
            pltpu.VMEM((length, 2 * length), BF16),
            pltpu.VMEM((2, length, length), F32),
            pltpu.VMEM((2, length, length), F32),
            sides,
            pltpu.VMEM((2, 2, length, tile), F32),
            packs, sides, packs,
            pltpu.VMEM((2, 2, rows_all, tile), BF16),
            pltpu.VMEM((2, 2, tile, tile), F32),
            pltpu.VMEM((2, 2, 2, tile, tile), BF16),
            pltpu.VMEM((2, 2, 2, tile // 2, tile), BF16),
            pltpu.SemaphoreType.DMA((5, 2, 4)),
            pltpu.SemaphoreType.DMA((5, 2, 4)),
            pltpu.SemaphoreType.DMA((5,)),
        ],
        compiler_params=pltpu.CompilerParams(
            collective_id=0, has_side_effects=True, vmem_limit_bytes=63 * 1024 * 1024
        ),
    )(
        offsets, owned, object_slices, probe,
        measured, tables,
    )


def solution(mesh):
    in_specs = (
        P(None, None, ("groups", "row"), "col"),
        P(),
        P(("groups", "row"), "col", None, None, None),
        P(("groups", "row"), "col", None, None),
        P(("groups", "row"), "col"),
    )
    out_specs = P(None, None, ("groups", "row"), "col")
    body = functools.partial(shards, mesh.shape["row"], mesh.shape["col"])
    return jax.shard_map(body, mesh=mesh, in_specs=in_specs, out_specs=out_specs, check_vma=False)
```
